32 devices in a mesh: slot: 4 (over y, x), tile: 8 (over z, core).
Axes of the slice: x: 2, y: 2, z: 4, core: 2. Of those that a mesh axis runs over, the one named last changes fastest.
Arguments:
- control: float32 [1024], replicated, may hold values from -6 to 6
- anomalies: bfloat16 [4, 64, 262144], P('slot', None, 'tile'), may hold values from -0.75 to 0.75
- modes: bfloat16 [16, 262144], P(None, 'tile'), may hold values from -1.5 to 1.5
- interp: bfloat16 [4, 1024, 128, 128], P('slot', 'tile'), may hold values from -0.5 to 0.5
- block_index: int32 [4, 1024], P('slot', 'tile'), may hold values from 0 to 2047
- counts: int32 [4, 8], P('slot', 'tile'), may hold values from 64 to 128, as said below
- innovation: float32 [4, 1024, 128], P('slot', 'tile'), may hold values from -6 to 6
- obs_weight: float32 [4, 1024, 128], P('slot', 'tile'), may hold values from 0.005 to 0.05
Outputs:
- departure: float32 [4, 1024, 128], P('slot', 'tile')
- gradient: float32 [1024], P('tile')
The draws below stay inside these ranges and needn't reach their ends.
Inputs may be any that keep to these rules, and one draw needn't show every extreme that they name: Only the first counts[g, j] of the 128 block slots of a device are observations; the others are ignored. Some device has all 128 live in every draw.
All inputs are finite; a program needn't handle non-finite values.
Results may differ from the reference program's by a relative error of at most 0.0027.
Values may be sent and summed in bfloat16 or wider, within the bound.
A program may use at most 64 MiB of HBM per device.

```python
import math
import jax
import jax.numpy as jnp
from jax import lax

K = 64
L = 16
M = 1024
BLK = 128
SB_DEV = 256
OB_DEV = 128
HB = 128
WIN = 512
SLOTS = 4
TILES = 8
NB = 2048
STATE = 262144
OBS_TILE = 1024


def draw_counts(key, part):
    key_one, key_two, key_three = jax.random.split(jax.random.fold_in(key, 17), 3)
    first_draw = jax.random.randint(key_one, (SLOTS, TILES), 0, OB_DEV + 1)
    second_draw = jax.random.randint(key_two, (SLOTS, TILES), 0, OB_DEV + 1)
    base_counts = jnp.maximum(first_draw * second_draw // OB_DEV, OB_DEV // 2)
    full_spot = jax.random.randint(key_three, (), 0, SLOTS * TILES)
    flat_counts = jnp.where(jnp.arange(SLOTS * TILES) == full_spot, OB_DEV, base_counts.reshape(-1))
    return flat_counts.reshape(SLOTS, TILES).astype(jnp.int32)


def place_ends(drawn, stream_key, smallest, top_value):
    shape = drawn.shape
    spot = [jax.random.randint(jax.random.fold_in(stream_key, axis), (), 0, shape[axis]) for axis in range(len(shape))]
    drawn = drawn.at[tuple(spot)].set(smallest)
    longest = shape.index(max(shape))
    spot[longest] = (spot[longest] + 1) % shape[longest]
    return drawn.at[tuple(spot)].set(top_value)


def block_scale(own_key, dims, shards, least, largest):
    gain = 1.0
    for axis_at, shards_of in shards:
        heights = jax.random.uniform(jax.random.fold_in(jax.random.fold_in(own_key, 6), axis_at), (shards_of,), jnp.float32, least / len(shards), largest / len(shards))
        gain = gain * jnp.repeat(jnp.exp(heights), dims[axis_at] // shards_of).reshape((-1,) + (1,) * (len(dims) - 1 - axis_at))
    return gain


def gaussian(stream_key, shape, spread, limit, cuts=(), held_as=jnp.bfloat16):
    values = jax.random.normal(stream_key, shape, jnp.float32) * spread
    if len(cuts) > 0:
        values = block_scale(stream_key, shape, cuts, -0.22, 0.18) * values
    return jnp.clip(values, min=-limit, max=limit).astype(held_as)


def setup_inputs(seed: int = 0) -> dict:
    arg_keys = jax.random.split(jax.random.key(seed), 9)
    control = gaussian(arg_keys[0], (M,), 1.0, 6.0, (), jnp.float32)
    anomalies = gaussian(arg_keys[1], (SLOTS, K, STATE), 0.125, 0.75, ((0, 4), (2, 8)))
    modes = gaussian(arg_keys[2], (L, STATE), 0.25, 1.5, ((1, 8),))
    interp = gaussian(arg_keys[3], (SLOTS, OBS_TILE, BLK, BLK), BLK ** -0.5, 0.5, ((0, 4), (1, 8)))
    block_index = place_ends(jax.random.randint(arg_keys[4], (SLOTS, OBS_TILE), 0, SLOTS * WIN), jax.random.fold_in(arg_keys[4], 1), 0, (SLOTS * WIN) - 1).astype(jnp.int32)
    counts = draw_counts(jax.random.fold_in(arg_keys[8], 71), 0)
    innovation = gaussian(arg_keys[6], (SLOTS, OBS_TILE, BLK), 1.0, 6.0, ((0, 4), (1, 8)), jnp.float32)
    obs_weight = jnp.clip(jnp.exp(math.log(0.05) - 2.3025851 * jax.random.uniform(arg_keys[7], (SLOTS, OBS_TILE, BLK), jnp.float32) ** block_scale(arg_keys[7], (SLOTS, OBS_TILE, BLK), ((0, 4), (1, 8)), -0.2, 0.2)), 0.005, 0.05)
    return {"control": control, "anomalies": anomalies, "modes": modes, "interp": interp, "block_index": block_index, "counts": counts, "innovation": innovation, "obs_weight": obs_weight}


def reference(control, anomalies, modes, interp, block_index, counts, innovation, obs_weight):
    coarse = control.astype(jnp.bfloat16).reshape(K, L)
    coefficients = jnp.dot(coarse, modes, preferred_element_type=jnp.float32)

    def increment_of(member_rows):
        return jnp.sum(member_rows.astype(jnp.float32) * coefficients, axis=0).astype(jnp.bfloat16)

    increments = lax.map(increment_of, anomalies)
    state_blocks = increments.reshape(SLOTS, NB, BLK)
    positions = jnp.arange(OBS_TILE, dtype=jnp.int32)
    tile_of = positions // OB_DEV
    block_rank = positions % OB_DEV

    def observe(inputs):
        block_mats, block_picks, tile_counts, targets, scales = inputs
        time_of = (block_picks // WIN).astype(jnp.int32)
        near_block = block_picks % WIN
        global_block = ((tile_of * SB_DEV - HB + near_block) % NB).astype(jnp.int32)
        block_states = state_blocks[time_of, global_block]
        mapped = jnp.einsum("bij,bj->bi", block_mats.astype(jnp.float32), block_states.astype(jnp.float32))
        live_mask = block_rank < tile_counts[tile_of]
        misfit = jnp.where(live_mask[:, None], mapped - targets, jnp.zeros_like(mapped))
        weighted = (scales * misfit).astype(jnp.bfloat16)
        pulled = jnp.einsum("bij,bi->bj", block_mats.astype(jnp.float32), weighted.astype(jnp.float32))
        return misfit, pulled, time_of, global_block

    departure, pulled, time_of, global_block = lax.map(observe, (interp, block_index, counts, innovation, obs_weight))
    adjoint = jnp.zeros((SLOTS, NB, BLK), jnp.float32).at[time_of, global_block].add(pulled)
    adjoint = adjoint.reshape(SLOTS, STATE)

    def project(inputs):
        member_rows, adjoint_row = inputs
        scaled = (adjoint_row[None, :] * modes.astype(jnp.float32)).astype(jnp.bfloat16)
        return jnp.dot(member_rows, scaled.T, preferred_element_type=jnp.float32)

    partials = lax.map(project, (anomalies, adjoint))
    gradient = control + jnp.sum(partials, axis=0).reshape(M)
    return departure, gradient
```

```python
import functools

import jax
import jax.numpy as jnp
from jax import lax
from jax.experimental import pallas as pl
from jax.experimental.pallas import tpu as pltpu
from jax.sharding import PartitionSpec as P

BLK = 128
HB = 128
STEP = 16
MESH = pl.DeviceIdType.MESH
NT = (((1,), (1,)), ((), ()))


def kernel(
    slots,
    tiles,
    ctl_ref,
    idx_ref,
    cnt_ref,
    anom_hbm,
    modes_hbm,
    interp_hbm,
    innov_hbm,
    wt_hbm,
    dep_hbm,
    grad_ref,
    anom,
    modes,
    interp,
    innov,
    wt,
    dep,
    coarse,
    idxs,
    pick_hot,
    add_hot,
    win,
    picks,
    got,
    states,
    pulled,
    edge_out,
    edge_in,
    adj,
    gs,
    gr,
    g2,
    local_sem,
    idx_sem,
    edge_sem,
    pick_sem,
    pull_sem,
    back_sem,
    g1_sem,
    g2_sem,
):
    s = lax.axis_index("slot")
    t = lax.axis_index("tile")
    members, rows = anom.shape
    width = modes.shape[0]
    blocks = rows // BLK
    obs = interp.shape[0]
    reach = blocks + 2 * HB
    parts = 4
    part_rows = rows // parts
    f32 = jnp.float32
    bf16 = jnp.bfloat16
    lower = lax.rem(t + tiles - 1, tiles)
    upper = lax.rem(t + 1, tiles)

    def slot_plus(d):
        return (lax.rem(s + d, slots), t)

    def slot_minus(d):
        return (lax.rem(s + slots - d, slots), t)

    def remote(src, dst, sems, i, target):
        return pltpu.make_async_remote_copy(
            src_ref=src,
            dst_ref=dst,
            send_sem=sems.at[0, i],
            recv_sem=sems.at[1, i],
            device_id=target,
            device_id_type=MESH,
        )

    loads = []
    for c in range(parts):
        cols = pl.ds(c * part_rows, part_rows)
        pair = (
            pltpu.make_async_copy(modes_hbm.at[:, cols], modes.at[:, cols], local_sem.at[2 * c]),
            pltpu.make_async_copy(anom_hbm.at[:, cols], anom.at[:, cols], local_sem.at[2 * c + 1]),
        )
        for copy in pair:
            copy.start()
        loads.append(pair)
    base = 2 * parts
    load_interp = pltpu.make_async_copy(interp_hbm, interp, local_sem.at[base])
    load_innov = pltpu.make_async_copy(innov_hbm, innov, local_sem.at[base + 1])
    load_wt = pltpu.make_async_copy(wt_hbm, wt, local_sem.at[base + 2])
    load_interp.start()
    load_innov.start()
    load_wt.start()

    barrier = pltpu.get_barrier_semaphore()
    for d in range(1, slots):
        pl.semaphore_signal(barrier, inc=1, device_id=slot_plus(d), device_id_type=MESH)
    for e in range(1, tiles):
        pl.semaphore_signal(
            barrier, inc=1, device_id=(s, lax.rem(t + e, tiles)), device_id_type=MESH
        )

    idxs[0] = jnp.broadcast_to(idx_ref[...], (8, BLK))

    per_row = BLK // width
    ctl = ctl_ref[...].astype(bf16)
    crows = ctl.shape[0]
    spread = (
        lax.broadcasted_iota(jnp.int32, (members, crows), 0) // per_row
        == lax.broadcasted_iota(jnp.int32, (members, crows), 1)
    )
    spread = jnp.where(spread, 1.0, 0.0).astype(bf16)
    wide = jnp.dot(spread, ctl, preferred_element_type=f32)
    lane = lax.broadcasted_iota(jnp.int32, (members, BLK), 1)
    member = lax.broadcasted_iota(jnp.int32, (members, BLK), 0)
    wide = jnp.where(lane // width == lax.rem(member, per_row), wide, 0.0).astype(bf16)
    fold = (
        lax.rem(lax.broadcasted_iota(jnp.int32, (width, BLK), 1), width)
        == lax.broadcasted_iota(jnp.int32, (width, BLK), 0)
    )
    fold = jnp.where(fold, 1.0, 0.0).astype(bf16)
    coarse[...] = lax.dot_general(fold, wide, NT, preferred_element_type=f32).astype(bf16)

    pl.semaphore_wait(barrier, slots - 1 + tiles - 1)

    idx_copies = []
    for d in range(1, slots):
        copy = remote(idxs.at[0], idxs.at[d], idx_sem, d, slot_plus(d))
        copy.start()
        idx_copies.append(copy)

    def increments(c):
        def body(i, carry):
            cols = pl.ds(pl.multiple_of(c * part_rows + i * (STEP * BLK), STEP * BLK), STEP * BLK)
            mixed = jnp.dot(coarse[...], anom[:, cols], preferred_element_type=f32)
            prod = mixed * modes[:, cols].astype(f32)
            sums = jnp.concatenate(
                [
                    jnp.sum(prod[:, j * BLK : (j + 1) * BLK], axis=0, keepdims=True)
                    for j in range(STEP)
                ],
                axis=0,
            )
            first = pl.multiple_of(HB + c * (part_rows // BLK) + i * STEP, STEP)
            win[pl.ds(first, STEP), :] = sums.astype(bf16)
            return carry

        lax.fori_loop(0, part_rows // (STEP * BLK), body, 0)

    for c in range(parts // 2):
        for copy in loads[c]:
            copy.wait()
        increments(c)
    to_lower = remote(
        win.at[pl.ds(HB, HB)], win.at[pl.ds(HB + blocks, HB)], edge_sem, 0, (s, lower)
    )
    to_lower.start()
    for c in range(parts // 2, parts):
        for copy in loads[c]:
            copy.wait()
        increments(c)
    to_upper = remote(win.at[pl.ds(blocks, HB)], win.at[pl.ds(0, HB)], edge_sem, 1, (s, upper))
    to_upper.start()

    origin = s * reach
    for d in range(slots):
        if d > 0:
            idx_copies[d - 1].wait_recv()
        row = idxs[d, 0:1, :]
        shifted = jnp.broadcast_to((row - origin).astype(f32), (obs, BLK))
        column = jnp.transpose(shifted)
        for q in range(reach // BLK):
            at = (lax.broadcasted_iota(jnp.int32, (obs, BLK), 1) + q * BLK).astype(f32)
            pick_hot[d, :, q * BLK : (q + 1) * BLK] = jnp.where(column == at, 1.0, 0.0).astype(bf16)
            at = (lax.broadcasted_iota(jnp.int32, (BLK, obs), 0) + q * BLK).astype(f32)
            add_hot[q * BLK : (q + 1) * BLK, d * obs : (d + 1) * obs] = jnp.where(
                shifted == at, 1.0, 0.0
            ).astype(bf16)

    to_lower.wait_recv()
    to_upper.wait_recv()

    pick_copies = []
    for d in range(1, slots):
        picks[d] = jnp.dot(pick_hot[d], win[...], preferred_element_type=f32).astype(bf16)
        copy = remote(picks.at[d], got.at[d], pick_sem, d, slot_minus(d))
        copy.start()
        pick_copies.append(copy)
    total = jnp.dot(pick_hot[0], win[...], preferred_element_type=f32)
    load_interp.wait()
    load_innov.wait()
    load_wt.wait()
    for d in range(1, slots):
        pick_copies[d - 1].wait_recv()
        total = total + got[d].astype(f32)
    states[...] = total.astype(bf16)

    live = cnt_ref[0, 0]
    sub = lax.broadcasted_iota(jnp.int32, (STEP, BLK), 0)

    def observe(g, carry):
        first = pl.multiple_of(g * STEP, STEP)
        mats = interp[pl.ds(first, STEP)].reshape(STEP * BLK, BLK)
        mapped_all = lax.dot_general(
            states[pl.ds(first, STEP), :], mats, NT, preferred_element_type=f32
        )
        mapped = mapped_all[:, 0:BLK]
        for r in range(1, STEP):
            mapped = jnp.where(sub == r, mapped_all[:, r * BLK : (r + 1) * BLK], mapped)
        misfit = jnp.where(
            sub + first < live, mapped - innov[pl.ds(first, STEP), :], jnp.zeros_like(mapped)
        )
        dep[pl.ds(first, STEP), :] = misfit
        weighted = wt[pl.ds(first, STEP), :] * misfit
        spread_w = jnp.concatenate(
            [jnp.where(sub == r, weighted, 0.0).astype(bf16) for r in range(STEP)], axis=1
        )
        pulled[pl.ds(first, STEP), :] = jnp.dot(
            spread_w, mats, preferred_element_type=f32
        ).astype(bf16)
        return carry

    lax.fori_loop(0, obs // STEP, observe, 0)

    pull_copies = []
    for d in range(1, slots):
        copy = remote(
            pulled.at[pl.ds(0, obs)], pulled.at[pl.ds(d * obs, obs)], pull_sem, d, slot_plus(d)
        )
        copy.start()
        pull_copies.append(copy)
    store_dep = pltpu.make_async_copy(dep, dep_hbm, local_sem.at[base + 3])
    store_dep.start()
    for copy in pull_copies:
        copy.wait_recv()

    edge_out[0] = jnp.dot(add_hot[0:HB, :], pulled[...], preferred_element_type=f32).astype(bf16)
    back_lower = remote(edge_out.at[0], edge_in.at[1], back_sem, 0, (s, lower))
    back_lower.start()
    edge_out[1] = jnp.dot(
        add_hot[HB + blocks : reach, :], pulled[...], preferred_element_type=f32
    ).astype(bf16)
    back_upper = remote(edge_out.at[1], edge_in.at[0], back_sem, 1, (s, upper))
    back_upper.start()
    adj[...] = jnp.dot(add_hot[HB : HB + blocks, :], pulled[...], preferred_element_type=f32)
    back_lower.wait_recv()
    back_upper.wait_recv()
    adj[0:HB, :] = adj[0:HB, :] + edge_in[0].astype(f32)
    adj[blocks - HB : blocks, :] = adj[blocks - HB : blocks, :] + edge_in[1].astype(f32)

    def project(i, acc):
        cols = pl.ds(pl.multiple_of(i * (STEP * BLK), STEP * BLK), STEP * BLK)
        rows_adj = adj[pl.ds(pl.multiple_of(i * STEP, STEP), STEP), :]
        part = modes[:, cols].astype(f32)
        scaled = jnp.concatenate(
            [
                (part[:, j * BLK : (j + 1) * BLK] * rows_adj[j : j + 1, :]).astype(bf16)
                for j in range(STEP)
            ],
            axis=1,
        )
        return acc + lax.dot_general(anom[:, cols], scaled, NT, preferred_element_type=f32)

    acc = lax.fori_loop(0, blocks // STEP, project, jnp.zeros((members, width), f32))

    share_rows = members // tiles
    wide = jnp.concatenate([acc] * per_row, axis=1)
    wide = jnp.where(lane // width == lax.rem(member, share_rows), wide, 0.0)
    for j in range(tiles):
        gs[j] = jnp.sum(wide[j * share_rows : (j + 1) * share_rows, :], axis=0, keepdims=True)

    g1_copies = []
    for e in range(1, tiles):
        to = lax.rem(t + e, tiles)
        copy = remote(gs.at[to], gr.at[e], g1_sem, e, (s, to))
        copy.start()
        g1_copies.append(copy)
    share = gs[t]
    for e in range(1, tiles):
        g1_copies[e - 1].wait_recv()
        share = share + gr[e]
    g2[0] = share
    g2_copies = []
    for d in range(1, slots):
        copy = remote(g2.at[0], g2.at[d], g2_sem, d, slot_plus(d))
        copy.start()
        g2_copies.append(copy)
    for d in range(1, slots):
        g2_copies[d - 1].wait_recv()
        share = share + g2[d]
    grad_ref[...] = share

    store_dep.wait()
    for copy in (
        idx_copies
        + [to_lower, to_upper]
        + pick_copies
        + pull_copies
        + [back_lower, back_upper]
        + g1_copies
        + g2_copies
    ):
        copy.wait_send()


def on_device(
    slots, tiles, control, anomalies, modes, interp, block_index, counts, innovation, obs_weight
):
    members, rows = anomalies.shape[1:]
    width = modes.shape[0]
    obs = interp.shape[1]
    blocks = rows // BLK
    reach = blocks + 2 * HB
    f32 = jnp.float32
    bf16 = jnp.bfloat16
    vmem = pl.BlockSpec(memory_space=pltpu.VMEM)
    hbm = pl.BlockSpec(memory_space=pl.ANY)

    def sems(n):
        return pltpu.SemaphoreType.DMA((2, n))

    departure, grad = pl.pallas_call(
        functools.partial(kernel, slots, tiles),
        out_shape=(
            jax.ShapeDtypeStruct((obs, BLK), f32),
            jax.ShapeDtypeStruct((1, BLK), f32),
        ),
        in_specs=[vmem, vmem, pl.BlockSpec(memory_space=pltpu.SMEM)] + [hbm] * 5,
        out_specs=(hbm, vmem),
        scratch_shapes=[
            pltpu.VMEM((members, rows), bf16),
            pltpu.VMEM((width, rows), bf16),
            pltpu.VMEM((obs, BLK, BLK), bf16),
            pltpu.VMEM((obs, BLK), f32),
            pltpu.VMEM((obs, BLK), f32),
            pltpu.VMEM((obs, BLK), f32),
            pltpu.VMEM((width, members), bf16),
            pltpu.VMEM((slots, 8, BLK), jnp.int32),
            pltpu.VMEM((slots, obs, reach), bf16),
            pltpu.VMEM((reach, slots * obs), bf16),
            pltpu.VMEM((reach, BLK), bf16),
            pltpu.VMEM((slots, obs, BLK), bf16),
            pltpu.VMEM((slots, obs, BLK), bf16),
            pltpu.VMEM((obs, BLK), bf16),
            pltpu.VMEM((slots * obs, BLK), bf16),
            pltpu.VMEM((2, HB, BLK), bf16),
            pltpu.VMEM((2, HB, BLK), bf16),
            pltpu.VMEM((blocks, BLK), f32),
            pltpu.VMEM((tiles, 1, BLK), f32),
            pltpu.VMEM((tiles, 1, BLK), f32),
            pltpu.VMEM((slots, 1, BLK), f32),
            pltpu.SemaphoreType.DMA((12,)),
            sems(slots),
            sems(2),
            sems(slots),
            sems(slots),
            sems(2),
            sems(tiles),
            sems(slots),
        ],
        compiler_params=pltpu.CompilerParams(
            collective_id=0, has_side_effects=True, vmem_limit_bytes=56 * 1024 * 1024
        ),
    )(
        control.reshape(-1, BLK),
        block_index,
        counts,
        anomalies[0],
        modes,
        interp[0],
        innovation[0],
        obs_weight[0],
    )
    share = control.shape[0] // tiles
    start = lax.axis_index("tile") * share
    gradient = lax.dynamic_slice_in_dim(control, start, share, 0) + grad[0, :share]
    return departure[None], gradient


def solution(mesh):
    in_specs = (
        P(),
        P("slot", None, "tile"),
        P(None, "tile"),
        P("slot", "tile", None, None),
        P("slot", "tile"),
        P("slot", "tile"),
        P("slot", "tile", None),
        P("slot", "tile", None),
    )
    out_specs = (P("slot", "tile", None), P("tile"))
    return jax.shard_map(
        functools.partial(on_device, mesh.shape["slot"], mesh.shape["tile"]),
        mesh=mesh,
        in_specs=in_specs,
        out_specs=out_specs,
        check_vma=False,
    )
```

```python
import functools

import jax
import jax.numpy as jnp
from jax import lax
from jax.experimental import pallas as pl
from jax.experimental.pallas import tpu as pltpu
from jax.sharding import PartitionSpec as P

BLK = 128
HB = 128
STEP = 16
MESH = pl.DeviceIdType.MESH
NT = (((1,), (1,)), ((), ()))


def kernel(
    slots,
    tiles,
    ctl_ref,
    idx_ref,
    cnt_ref,
    anom_hbm,
    modes_hbm,
    interp_hbm,
    innov_hbm,
    wt_hbm,
    dep_hbm,
    grad_ref,
    anom,
    modes,
    interp,
    innov,
    wt,
    dep,
    coarse,
    idxs,
    pick_hot,
    add_hot,
    edge_pick,
    edge_add,
    win,
    edges,
    picks,
    got,
    states,
    pulled,
    edge_out,
    edge_back,
    inner_out,
    inner_back,
    adj,
    gs,
    gp,
    gr,
    local_sem,
    idx_sem,
    edge_sem,
    core_sem,
    pick_sem,
    pull_sem,
    back_sem,
    g_sem,
):
    s = lax.axis_index("slot")
    t = lax.axis_index("tile")
    members, rows = anom.shape
    width = modes.shape[0]
    blocks = rows // BLK
    obs = interp.shape[0]
    reach = blocks + 2 * HB
    f32 = jnp.float32
    bf16 = jnp.bfloat16
    chips = tiles // 2
    z = t // 2
    core = lax.rem(t, 2)
    partner = (s, t + 1 - 2 * core)
    outer = lax.rem(t + tiles - 1 + 2 * core, tiles)
    halves = (core, 1 - core)

    def slot_plus(d, tile=None):
        return (lax.rem(s + d, slots), t if tile is None else tile)

    def slot_minus(d):
        return (lax.rem(s + slots - d, slots), t)

    def remote(src, dst, sems, i, target):
        return pltpu.make_async_remote_copy(
            src_ref=src,
            dst_ref=dst,
            send_sem=sems.at[0, i],
            recv_sem=sems.at[1, i],
            device_id=target,
            device_id_type=MESH,
        )

    parts = 4
    part_rows = rows // parts
    starts = [
        pl.multiple_of(half * (rows // 2) + q * part_rows, part_rows)
        for half in halves
        for q in range(2)
    ]
    loads = []
    for c in range(parts):
        cols = pl.ds(starts[c], part_rows)
        pair = (
            pltpu.make_async_copy(modes_hbm.at[:, cols], modes.at[:, cols], local_sem.at[2 * c]),
            pltpu.make_async_copy(anom_hbm.at[:, cols], anom.at[:, cols], local_sem.at[2 * c + 1]),
        )
        for copy in pair:
            copy.start()
        loads.append(pair)
    base = 2 * parts
    load_interp = pltpu.make_async_copy(interp_hbm, interp, local_sem.at[base])
    load_innov = pltpu.make_async_copy(innov_hbm, innov, local_sem.at[base + 1])
    load_wt = pltpu.make_async_copy(wt_hbm, wt, local_sem.at[base + 2])
    load_interp.start()
    load_innov.start()
    load_wt.start()

    barrier = pltpu.get_barrier_semaphore()
    pl.semaphore_signal(barrier, inc=1, device_id=partner, device_id_type=MESH)
    greeted = 1
    for d in range(slots):
        for e in range(chips):
            if d or e:
                to = (lax.rem(s + d, slots), lax.rem(z + e, chips) * 2 + core)
                pl.semaphore_signal(barrier, inc=1, device_id=to, device_id_type=MESH)
                greeted += 1
    for d in range(slots):
        pl.semaphore_signal(barrier, inc=1, device_id=slot_plus(d, outer), device_id_type=MESH)
        greeted += 1

    idxs[0] = jnp.broadcast_to(idx_ref[...], (8, BLK))

    per_row = BLK // width
    ctl = ctl_ref[...].astype(bf16)
    crows = ctl.shape[0]
    spread = (
        lax.broadcasted_iota(jnp.int32, (members, crows), 0) // per_row
        == lax.broadcasted_iota(jnp.int32, (members, crows), 1)
    )
    spread = jnp.where(spread, 1.0, 0.0).astype(bf16)
    wide = jnp.dot(spread, ctl, preferred_element_type=f32)
    lane = lax.broadcasted_iota(jnp.int32, (members, BLK), 1)
    member = lax.broadcasted_iota(jnp.int32, (members, BLK), 0)
    wide = jnp.where(lane // width == lax.rem(member, per_row), wide, 0.0).astype(bf16)
    fold = (
        lax.rem(lax.broadcasted_iota(jnp.int32, (width, BLK), 1), width)
        == lax.broadcasted_iota(jnp.int32, (width, BLK), 0)
    )
    fold = jnp.where(fold, 1.0, 0.0).astype(bf16)
    coarse[...] = lax.dot_general(fold, wide, NT, preferred_element_type=f32).astype(bf16)

    half_blocks = blocks // 2
    half_at = [pl.multiple_of(half * half_blocks, half_blocks) for half in halves]

    def increments(h, q):
        def body(i, carry):
            block = half_at[h] + q * (half_blocks // 2) + i * STEP
            block = pl.multiple_of(block, STEP)
            cols = pl.ds(pl.multiple_of(block * BLK, STEP * BLK), STEP * BLK)
            mixed = jnp.dot(coarse[...], anom[:, cols], preferred_element_type=f32)
            prod = mixed * modes[:, cols].astype(f32)
            sums = jnp.concatenate(
                [
                    jnp.sum(prod[:, j * BLK : (j + 1) * BLK], axis=0, keepdims=True)
                    for j in range(STEP)
                ],
                axis=0,
            )
            win[pl.ds(block, STEP), :] = sums.astype(bf16)
            return carry

        lax.fori_loop(0, half_blocks // 2 // STEP, body, 0)

    for q in range(2):
        for copy in loads[q]:
            copy.wait()
        increments(0, q)

    pl.semaphore_wait(barrier, greeted)

    idx_copies = []
    for d in range(1, slots):
        copy = remote(idxs.at[0], idxs.at[d], idx_sem, d, slot_plus(d))
        copy.start()
        idx_copies.append(copy)
    edge_copies = []
    for d in range(slots):
        copy = remote(
            win.at[pl.ds(half_at[0], HB)],
            edges.at[pl.ds(d * HB, HB)],
            edge_sem,
            d,
            slot_plus(d, outer),
        )
        copy.start()
        edge_copies.append(copy)

    for q in range(2):
        for copy in loads[2 + q]:
            copy.wait()
        increments(1, q)
    inner_copy = remote(
        win.at[pl.ds(half_at[1], HB)], win.at[pl.ds(blocks, HB)], core_sem, 0, partner
    )
    inner_copy.start()

    origin = s * reach
    outer_at = core * (HB + blocks)
    inner_at = HB + blocks - outer_at
    along = lax.broadcasted_iota(jnp.int32, (obs, BLK), 1)
    down = lax.broadcasted_iota(jnp.int32, (BLK, obs), 0)

    def hot(condition):
        return jnp.where(condition, 1.0, 0.0).astype(bf16)

    mine = jnp.broadcast_to(idxs[0, 0:1, :].astype(f32), (obs, BLK))
    mine_column = jnp.transpose(mine)
    for d in range(slots):
        at = lax.rem(s + slots - d, slots) * reach + outer_at
        edge_pick[:, d * HB : (d + 1) * HB] = hot(mine_column == (along + at).astype(f32))
        edge_add[d * HB : (d + 1) * HB, :] = hot(mine == (down + at).astype(f32))
    for d in range(slots):
        if d > 0:
            idx_copies[d - 1].wait_recv()
        listed = jnp.broadcast_to(idxs[d, 0:1, :].astype(f32), (obs, BLK))
        column = jnp.transpose(listed)
        for q in range(blocks // BLK + 1):
            at = origin + (HB + q * BLK if q < blocks // BLK else inner_at)
            pick_hot[d, :, q * BLK : (q + 1) * BLK] = hot(column == (along + at).astype(f32))
            add_hot[q * BLK : (q + 1) * BLK, d * obs : (d + 1) * obs] = hot(
                listed == (down + at).astype(f32)
            )

    inner_copy.wait_recv()
    pick_copies = []
    for d in range(1, slots):
        picks[d] = jnp.dot(pick_hot[d], win[...], preferred_element_type=f32).astype(bf16)
        copy = remote(picks.at[d], got.at[d], pick_sem, d, slot_minus(d))
        copy.start()
        pick_copies.append(copy)
    total = jnp.dot(pick_hot[0], win[...], preferred_element_type=f32)
    load_interp.wait()
    load_innov.wait()
    load_wt.wait()
    for copy in edge_copies:
        copy.wait_recv()
    total = total + jnp.dot(edge_pick[...], edges[...], preferred_element_type=f32)
    for d in range(1, slots):
        pick_copies[d - 1].wait_recv()
        total = total + got[d].astype(f32)
    states[...] = total.astype(bf16)

    live = cnt_ref[0, 0]
    sub = lax.broadcasted_iota(jnp.int32, (STEP, BLK), 0)

    def observe(g, carry):
        first = pl.multiple_of(g * STEP, STEP)
        mats = interp[pl.ds(first, STEP)].reshape(STEP * BLK, BLK)
        mapped_all = lax.dot_general(
            states[pl.ds(first, STEP), :], mats, NT, preferred_element_type=f32
        )
        mapped = mapped_all[:, 0:BLK]
        for r in range(1, STEP):
            mapped = jnp.where(sub == r, mapped_all[:, r * BLK : (r + 1) * BLK], mapped)
        misfit = jnp.where(
            sub + first < live, mapped - innov[pl.ds(first, STEP), :], jnp.zeros_like(mapped)
        )
        dep[pl.ds(first, STEP), :] = misfit
        weighted = wt[pl.ds(first, STEP), :] * misfit
        spread_w = jnp.concatenate(
            [jnp.where(sub == r, weighted, 0.0).astype(bf16) for r in range(STEP)], axis=1
        )
        pulled[pl.ds(first, STEP), :] = jnp.dot(
            spread_w, mats, preferred_element_type=f32
        ).astype(bf16)
        return carry

    lax.fori_loop(0, obs // STEP, observe, 0)

    pull_copies = []
    for d in range(1, slots):
        copy = remote(
            pulled.at[pl.ds(0, obs)], pulled.at[pl.ds(d * obs, obs)], pull_sem, d, slot_plus(d)
        )
        copy.start()
        pull_copies.append(copy)
    edge_out[...] = jnp.dot(
        edge_add[...], pulled[0:obs, :], preferred_element_type=f32
    ).astype(bf16)
    back_copies = []
    for d in range(slots):
        copy = remote(
            edge_out.at[pl.ds(d * HB, HB)],
            edge_back.at[d],
            back_sem,
            d,
            (lax.rem(s + slots - d, slots), outer),
        )
        copy.start()
        back_copies.append(copy)
    store_dep = pltpu.make_async_copy(dep, dep_hbm, local_sem.at[base + 3])
    store_dep.start()
    for copy in pull_copies:
        copy.wait_recv()

    inner_out[...] = jnp.dot(
        add_hot[blocks : blocks + HB, :], pulled[...], preferred_element_type=f32
    ).astype(bf16)
    inner_send = remote(inner_out, inner_back, core_sem, 1, partner)
    inner_send.start()
    adj[...] = jnp.dot(add_hot[0:blocks, :], pulled[...], preferred_element_type=f32)
    extra = None
    for d in range(slots):
        back_copies[d].wait_recv()
        got_edge = edge_back[d].astype(f32)
        extra = got_edge if extra is None else extra + got_edge
    outer_half = pl.ds(half_at[0], HB)
    adj[outer_half, :] = adj[outer_half, :] + extra

    def project(h):
        def body(i, acc):
            block = pl.multiple_of(half_at[h] + i * STEP, STEP)
            cols = pl.ds(pl.multiple_of(block * BLK, STEP * BLK), STEP * BLK)
            rows_adj = adj[pl.ds(block, STEP), :]
            part = modes[:, cols].astype(f32)
            scaled = jnp.concatenate(
                [
                    (part[:, j * BLK : (j + 1) * BLK] * rows_adj[j : j + 1, :]).astype(bf16)
                    for j in range(STEP)
                ],
                axis=1,
            )
            return acc + lax.dot_general(anom[:, cols], scaled, NT, preferred_element_type=f32)

        return body

    steps = half_blocks // STEP
    acc = lax.fori_loop(0, steps, project(0), jnp.zeros((members, width), f32))
    inner_send.wait_recv()
    inner_half = pl.ds(half_at[1], HB)
    adj[inner_half, :] = adj[inner_half, :] + inner_back[...].astype(f32)
    acc = lax.fori_loop(0, steps, project(1), acc)

    share_rows = members // tiles
    wide = jnp.concatenate([acc] * per_row, axis=1)
    wide = jnp.where(lane // width == lax.rem(member, share_rows), wide, 0.0)
    for j in range(tiles):
        gs[j % 2, j // 2] = jnp.sum(
            wide[j * share_rows : (j + 1) * share_rows, :], axis=0, keepdims=True
        )

    core_send = remote(gs.at[1 - core], gp, core_sem, 2, partner)
    core_send.start()
    core_send.wait_recv()
    gs[core] = gs[core] + gp[...]
    g_copies = []
    for d in range(slots):
        for e in range(chips):
            if d or e:
                to = lax.rem(z + e, chips)
                i = d * chips + e
                copy = remote(
                    gs.at[core, to],
                    gr.at[i],
                    g_sem,
                    i,
                    (lax.rem(s + d, slots), to * 2 + core),
                )
                copy.start()
                g_copies.append(copy)

    share = members * width // tiles
    per_line = BLK // share
    line = ctl_ref[pl.ds(t // per_line, 1), :]
    own = line
    for q in range(1, per_line):
        moved = jnp.concatenate([line[:, q * share :], line[:, : q * share]], axis=1)
        own = jnp.where(lax.rem(t, per_line) == q, moved, own)

    result = gs[core, z]
    for copy in g_copies:
        copy.wait_recv()
    for i in range(1, slots * chips):
        result = result + gr[i]
    grad_ref[...] = own + result

    store_dep.wait()
    for copy in (
        idx_copies
        + edge_copies
        + [inner_copy]
        + pick_copies
        + pull_copies
        + back_copies
        + [inner_send, core_send]
        + g_copies
    ):
        copy.wait_send()


def deliver(dep_in, grad_in, dep_out, grad_out, sem):
    pair = (
        pltpu.make_async_copy(dep_in, dep_out, sem.at[0]),
        pltpu.make_async_copy(grad_in, grad_out, sem.at[1]),
    )
    for copy in pair:
        copy.start()
    for copy in pair:
        copy.wait()


def on_device(
    slots, tiles, control, anomalies, modes, interp, block_index, counts, innovation, obs_weight
):
    members, rows = anomalies.shape[1:]
    width = modes.shape[0]
    obs = interp.shape[1]
    blocks = rows // BLK
    near = blocks + HB
    f32 = jnp.float32
    bf16 = jnp.bfloat16
    vmem = pl.BlockSpec(memory_space=pltpu.VMEM)
    hbm = pl.BlockSpec(memory_space=pl.ANY)

    def sems(n):
        return pltpu.SemaphoreType.DMA((2, n))

    departure, grad = pl.pallas_call(
        functools.partial(kernel, slots, tiles),
        out_shape=(
            jax.ShapeDtypeStruct((obs, BLK), f32),
            jax.ShapeDtypeStruct((1, BLK), f32),
        ),
        in_specs=[vmem, vmem, pl.BlockSpec(memory_space=pltpu.SMEM)] + [hbm] * 5,
        out_specs=(hbm, vmem),
        scratch_shapes=[
            pltpu.VMEM((members, rows), bf16),
            pltpu.VMEM((width, rows), bf16),
            pltpu.VMEM((obs, BLK, BLK), bf16),
            pltpu.VMEM((obs, BLK), f32),
            pltpu.VMEM((obs, BLK), f32),
            pltpu.VMEM((obs, BLK), f32),
            pltpu.VMEM((width, members), bf16),
            pltpu.VMEM((slots, 8, BLK), jnp.int32),
            pltpu.VMEM((slots, obs, near), bf16),
            pltpu.VMEM((near, slots * obs), bf16),
            pltpu.VMEM((obs, slots * HB), bf16),
            pltpu.VMEM((slots * HB, obs), bf16),
            pltpu.VMEM((near, BLK), bf16),
            pltpu.VMEM((slots * HB, BLK), bf16),
            pltpu.VMEM((slots, obs, BLK), bf16),
            pltpu.VMEM((slots, obs, BLK), bf16),
            pltpu.VMEM((obs, BLK), bf16),
            pltpu.VMEM((slots * obs, BLK), bf16),
            pltpu.VMEM((slots * HB, BLK), bf16),
            pltpu.VMEM((slots, HB, BLK), bf16),
            pltpu.VMEM((HB, BLK), bf16),
            pltpu.VMEM((HB, BLK), bf16),
            pltpu.VMEM((blocks, BLK), f32),
            pltpu.VMEM((2, tiles // 2, 1, BLK), f32),
            pltpu.VMEM((tiles // 2, 1, BLK), f32),
            pltpu.VMEM((slots * tiles // 2, 1, BLK), f32),
            pltpu.SemaphoreType.DMA((12,)),
            sems(slots),
            sems(slots),
            sems(3),
            sems(slots),
            sems(slots),
            sems(slots),
            sems(slots * tiles // 2),
        ],
        compiler_params=pltpu.CompilerParams(
            collective_id=0, has_side_effects=True, vmem_limit_bytes=56 * 1024 * 1024
        ),
    )(
        control.reshape(-1, BLK),
        block_index,
        counts,
        anomalies[0],
        modes,
        interp[0],
        innovation[0],
        obs_weight[0],
    )
    departure, grad = pl.pallas_call(
        deliver,
        out_shape=(
            jax.ShapeDtypeStruct((obs, BLK), f32),
            jax.ShapeDtypeStruct((1, BLK), f32),
        ),
        in_specs=[hbm] * 2,
        out_specs=(hbm, hbm),
        scratch_shapes=[pltpu.SemaphoreType.DMA((2,))],
    )(departure, grad)
    gradient = grad[0, : control.shape[0] // tiles]
    return departure[None], gradient


def solution(mesh):
    in_specs = (
        P(),
        P("slot", None, "tile"),
        P(None, "tile"),
        P("slot", "tile", None, None),
        P("slot", "tile"),
        P("slot", "tile"),
        P("slot", "tile", None),
        P("slot", "tile", None),
    )
    out_specs = (P("slot", "tile", None), P("tile"))
    return jax.shard_map(
        functools.partial(on_device, mesh.shape["slot"], mesh.shape["tile"]),
        mesh=mesh,
        in_specs=in_specs,
        out_specs=out_specs,
        check_vma=False,
    )
```

```python
import functools

import jax
import jax.numpy as jnp
from jax import lax
from jax.experimental import pallas as pl
from jax.experimental.pallas import tpu as pltpu
from jax.sharding import PartitionSpec as P

BLK = 128
HB = 128
STEP = 16
MESH = pl.DeviceIdType.MESH
NT = (((1,), (1,)), ((), ()))


def kernel(
    slots,
    tiles,
    ctl_ref,
    idx_ref,
    cnt_ref,
    anom_hbm,
    modes_hbm,
    interp_hbm,
    innov_hbm,
    wt_hbm,
    dep_ref,
    grad_ref,
    anom,
    modes,
    interp,
    innov,
    wt,
    coarse,
    idxs,
    pick_hot,
    add_hot,
    edge_pick,
    edge_add,
    win,
    edges,
    picks,
    got,
    states,
    pulled,
    edge_out,
    edge_back,
    inner_out,
    inner_back,
    adj,
    gs,
    gp,
    gr,
    local_sem,
    idx_sem,
    edge_sem,
    core_sem,
    pick_sem,
    pull_sem,
    back_sem,
    g_sem,
):
    s = lax.axis_index("slot")
    t = lax.axis_index("tile")
    members, rows = anom.shape
    width = modes.shape[0]
    blocks = rows // BLK
    obs = interp.shape[0]
    reach = blocks + 2 * HB
    f32 = jnp.float32
    bf16 = jnp.bfloat16
    chips = tiles // 2
    z = t // 2
    core = lax.rem(t, 2)
    partner = (s, t + 1 - 2 * core)
    outer = lax.rem(t + tiles - 1 + 2 * core, tiles)
    halves = (core, 1 - core)

    def slot_plus(d, tile=None):
        return (lax.rem(s + d, slots), t if tile is None else tile)

    def slot_minus(d):
        return (lax.rem(s + slots - d, slots), t)

    def remote(src, dst, sems, i, target):
        return pltpu.make_async_remote_copy(
            src_ref=src,
            dst_ref=dst,
            send_sem=sems.at[0, i],
            recv_sem=sems.at[1, i],
            device_id=target,
            device_id_type=MESH,
        )

    barrier = pltpu.get_barrier_semaphore()
    pl.semaphore_signal(barrier, inc=1, device_id=partner, device_id_type=MESH)
    greeted = 1
    for d in range(slots):
        for e in range(chips):
            if d or e:
                to = (lax.rem(s + d, slots), lax.rem(z + e, chips) * 2 + core)
                pl.semaphore_signal(barrier, inc=1, device_id=to, device_id_type=MESH)
                greeted += 1
    for d in range(slots):
        pl.semaphore_signal(barrier, inc=1, device_id=slot_plus(d, outer), device_id_type=MESH)
        greeted += 1

    parts = 4
    part_rows = rows // parts
    starts = [
        pl.multiple_of(half * (rows // 2) + q * part_rows, part_rows)
        for half in halves
        for q in range(2)
    ]
    loads = []
    for c in range(parts):
        cols = pl.ds(starts[c], part_rows)
        pair = (
            pltpu.make_async_copy(modes_hbm.at[:, cols], modes.at[:, cols], local_sem.at[2 * c]),
            pltpu.make_async_copy(anom_hbm.at[:, cols], anom.at[:, cols], local_sem.at[2 * c + 1]),
        )
        for copy in pair:
            copy.start()
        loads.append(pair)
    base = 2 * parts
    load_interp = pltpu.make_async_copy(interp_hbm, interp, local_sem.at[base])
    load_innov = pltpu.make_async_copy(innov_hbm, innov, local_sem.at[base + 1])
    load_wt = pltpu.make_async_copy(wt_hbm, wt, local_sem.at[base + 2])
    load_interp.start()
    load_innov.start()
    load_wt.start()

    idxs[0] = jnp.broadcast_to(idx_ref[...], (8, BLK))

    per_row = BLK // width
    ctl = ctl_ref[...].astype(bf16)
    crows = ctl.shape[0]
    spread = (
        lax.broadcasted_iota(jnp.int32, (members, crows), 0) // per_row
        == lax.broadcasted_iota(jnp.int32, (members, crows), 1)
    )
    spread = jnp.where(spread, 1.0, 0.0).astype(bf16)
    wide = jnp.dot(spread, ctl, preferred_element_type=f32)
    lane = lax.broadcasted_iota(jnp.int32, (members, BLK), 1)
    member = lax.broadcasted_iota(jnp.int32, (members, BLK), 0)
    wide = jnp.where(lane // width == lax.rem(member, per_row), wide, 0.0).astype(bf16)
    fold = (
        lax.rem(lax.broadcasted_iota(jnp.int32, (width, BLK), 1), width)
        == lax.broadcasted_iota(jnp.int32, (width, BLK), 0)
    )
    fold = jnp.where(fold, 1.0, 0.0).astype(bf16)
    coarse[...] = lax.dot_general(fold, wide, NT, preferred_element_type=f32).astype(bf16)

    half_blocks = blocks // 2
    half_at = [pl.multiple_of(half * half_blocks, half_blocks) for half in halves]

    def increments(h, q):
        def body(i, carry):
            block = half_at[h] + q * (half_blocks // 2) + i * STEP
            block = pl.multiple_of(block, STEP)
            cols = pl.ds(pl.multiple_of(block * BLK, STEP * BLK), STEP * BLK)
            mixed = jnp.dot(coarse[...], anom[:, cols], preferred_element_type=f32)
            prod = mixed * modes[:, cols].astype(f32)
            sums = jnp.concatenate(
                [
                    jnp.sum(prod[:, j * BLK : (j + 1) * BLK], axis=0, keepdims=True)
                    for j in range(STEP)
                ],
                axis=0,
            )
            win[pl.ds(block, STEP), :] = sums.astype(bf16)
            return carry

        lax.fori_loop(0, half_blocks // 2 // STEP, body, 0, unroll=2)

    for q in range(2):
        for copy in loads[q]:
            copy.wait()
        increments(0, q)

    pl.semaphore_wait(barrier, greeted)

    idx_copies = []
    for d in range(1, slots):
        copy = remote(idxs.at[0], idxs.at[d], idx_sem, d, slot_plus(d))
        copy.start()
        idx_copies.append(copy)
    edge_copies = []
    for d in range(slots):
        copy = remote(
            win.at[pl.ds(half_at[0], HB)],
            edges.at[pl.ds(d * HB, HB)],
            edge_sem,
            d,
            slot_plus(d, outer),
        )
        copy.start()
        edge_copies.append(copy)

    for q in range(2):
        for copy in loads[2 + q]:
            copy.wait()
        increments(1, q)
    inner_copy = remote(
        win.at[pl.ds(half_at[1], HB)], win.at[pl.ds(blocks, HB)], core_sem, 0, partner
    )
    inner_copy.start()

    origin = s * reach
    outer_at = core * (HB + blocks)
    inner_at = HB + blocks - outer_at
    along = lax.broadcasted_iota(jnp.int32, (obs, BLK), 1)
    down = lax.broadcasted_iota(jnp.int32, (BLK, obs), 0)

    def hot(condition):
        return jnp.where(condition, 1.0, 0.0).astype(bf16)

    mine = jnp.broadcast_to(idxs[0, 0:1, :].astype(f32), (obs, BLK))
    mine_column = jnp.transpose(mine)
    for d in range(slots):
        at = lax.rem(s + slots - d, slots) * reach + outer_at
        edge_pick[:, d * HB : (d + 1) * HB] = hot(mine_column == (along + at).astype(f32))
        edge_add[d * HB : (d + 1) * HB, :] = hot(mine == (down + at).astype(f32))
    for d in range(slots):
        if d > 0:
            idx_copies[d - 1].wait_recv()
        listed = jnp.broadcast_to(idxs[d, 0:1, :].astype(f32), (obs, BLK))
        column = jnp.transpose(listed)
        for q in range(blocks // BLK + 1):
            at = origin + (HB + q * BLK if q < blocks // BLK else inner_at)
            pick_hot[d, :, q * BLK : (q + 1) * BLK] = hot(column == (along + at).astype(f32))
            add_hot[q * BLK : (q + 1) * BLK, d * obs : (d + 1) * obs] = hot(
                listed == (down + at).astype(f32)
            )

    inner_copy.wait_recv()
    pick_copies = []
    for d in range(1, slots):
        picks[d] = jnp.dot(pick_hot[d], win[...], preferred_element_type=f32).astype(bf16)
        copy = remote(picks.at[d], got.at[d], pick_sem, d, slot_minus(d))
        copy.start()
        pick_copies.append(copy)
    total = jnp.dot(pick_hot[0], win[...], preferred_element_type=f32)
    load_interp.wait()
    load_innov.wait()
    load_wt.wait()
    for copy in edge_copies:
        copy.wait_recv()
    total = total + jnp.dot(edge_pick[...], edges[...], preferred_element_type=f32)
    for d in range(1, slots):
        pick_copies[d - 1].wait_recv()
        total = total + got[d].astype(f32)
    states[...] = total.astype(bf16)

    live = cnt_ref[0, 0]
    sub = lax.broadcasted_iota(jnp.int32, (STEP, BLK), 0)

    def observe(g, carry):
        first = pl.multiple_of(g * STEP, STEP)
        mats = interp[pl.ds(first, STEP)].reshape(STEP * BLK, BLK)
        mapped_all = lax.dot_general(
            states[pl.ds(first, STEP), :], mats, NT, preferred_element_type=f32
        )
        mapped = mapped_all[:, 0:BLK]
        for r in range(1, STEP):
            mapped = jnp.where(sub == r, mapped_all[:, r * BLK : (r + 1) * BLK], mapped)
        misfit = jnp.where(
            sub + first < live, mapped - innov[pl.ds(first, STEP), :], jnp.zeros_like(mapped)
        )
        dep_ref[pl.ds(first, STEP), :] = misfit
        weighted = wt[pl.ds(first, STEP), :] * misfit
        spread_w = jnp.concatenate(
            [jnp.where(sub == r, weighted, 0.0).astype(bf16) for r in range(STEP)], axis=1
        )
        pulled[pl.ds(first, STEP), :] = jnp.dot(
            spread_w, mats, preferred_element_type=f32
        ).astype(bf16)
        return carry

    lax.fori_loop(0, obs // STEP, observe, 0, unroll=4)

    pull_copies = []
    for d in range(1, slots):
        copy = remote(
            pulled.at[pl.ds(0, obs)], pulled.at[pl.ds(d * obs, obs)], pull_sem, d, slot_plus(d)
        )
        copy.start()
        pull_copies.append(copy)
    edge_out[...] = jnp.dot(
        edge_add[...], pulled[0:obs, :], preferred_element_type=f32
    ).astype(bf16)
    back_copies = []
    for d in range(slots):
        copy = remote(
            edge_out.at[pl.ds(d * HB, HB)],
            edge_back.at[d],
            back_sem,
            d,
            (lax.rem(s + slots - d, slots), outer),
        )
        copy.start()
        back_copies.append(copy)
    for copy in pull_copies:
        copy.wait_recv()

    inner_out[...] = jnp.dot(
        add_hot[blocks : blocks + HB, :], pulled[...], preferred_element_type=f32
    ).astype(bf16)
    inner_send = remote(inner_out, inner_back, core_sem, 1, partner)
    inner_send.start()
    adj[...] = jnp.dot(add_hot[0:blocks, :], pulled[...], preferred_element_type=f32)
    extra = None
    for d in range(slots):
        back_copies[d].wait_recv()
        got_edge = edge_back[d].astype(f32)
        extra = got_edge if extra is None else extra + got_edge
    outer_half = pl.ds(half_at[0], HB)
    adj[outer_half, :] = adj[outer_half, :] + extra

    def project(h):
        def body(i, acc):
            block = pl.multiple_of(half_at[h] + i * STEP, STEP)
            cols = pl.ds(pl.multiple_of(block * BLK, STEP * BLK), STEP * BLK)
            rows_adj = adj[pl.ds(block, STEP), :]
            part = modes[:, cols].astype(f32)
            scaled = jnp.concatenate(
                [
                    (part[:, j * BLK : (j + 1) * BLK] * rows_adj[j : j + 1, :]).astype(bf16)
                    for j in range(STEP)
                ],
                axis=1,
            )
            return acc + lax.dot_general(anom[:, cols], scaled, NT, preferred_element_type=f32)

        return body

    steps = half_blocks // STEP
    acc = lax.fori_loop(0, steps, project(0), jnp.zeros((members, width), f32), unroll=4)
    inner_send.wait_recv()
    inner_half = pl.ds(half_at[1], HB)
    adj[inner_half, :] = adj[inner_half, :] + inner_back[...].astype(f32)
    acc = lax.fori_loop(0, steps, project(1), acc, unroll=4)

    share_rows = members // tiles
    wide = jnp.concatenate([acc] * per_row, axis=1)
    wide = jnp.where(lane // width == lax.rem(member, share_rows), wide, 0.0)
    for j in range(tiles):
        gs[j % 2, j // 2] = jnp.sum(
            wide[j * share_rows : (j + 1) * share_rows, :], axis=0, keepdims=True
        )

    core_send = remote(gs.at[1 - core], gp, core_sem, 2, partner)
    core_send.start()
    core_send.wait_recv()
    gs[core] = gs[core] + gp[...]
    g_copies = []
    for d in range(slots):
        for e in range(chips):
            if d or e:
                to = lax.rem(z + e, chips)
                i = d * chips + e
                copy = remote(
                    gs.at[core, to],
                    gr.at[i],
                    g_sem,
                    i,
                    (lax.rem(s + d, slots), to * 2 + core),
                )
                copy.start()
                g_copies.append(copy)

    share = members * width // tiles
    per_line = BLK // share
    line = ctl_ref[pl.ds(t // per_line, 1), :]
    own = line
    for q in range(1, per_line):
        moved = jnp.concatenate([line[:, q * share :], line[:, : q * share]], axis=1)
        own = jnp.where(lax.rem(t, per_line) == q, moved, own)

    result = gs[core, z]
    for copy in g_copies:
        copy.wait_recv()
    for i in range(1, slots * chips):
        result = result + gr[i]
    grad_ref[...] = own + result

    for copy in (
        idx_copies
        + edge_copies
        + [inner_copy]
        + pick_copies
        + pull_copies
        + back_copies
        + [inner_send, core_send]
        + g_copies
    ):
        copy.wait_send()


def on_device(
    slots, tiles, control, anomalies, modes, interp, block_index, counts, innovation, obs_weight
):
    members, rows = anomalies.shape[1:]
    width = modes.shape[0]
    obs = interp.shape[1]
    blocks = rows // BLK
    near = blocks + HB
    f32 = jnp.float32
    bf16 = jnp.bfloat16
    vmem = pl.BlockSpec(memory_space=pltpu.VMEM)
    hbm = pl.BlockSpec(memory_space=pl.ANY)

    def sems(n):
        return pltpu.SemaphoreType.DMA((2, n))

    departure, grad = pl.pallas_call(
        functools.partial(kernel, slots, tiles),
        out_shape=(
            pltpu.VMEM((obs, BLK), f32),
            pltpu.VMEM((1, BLK), f32),
        ),
        in_specs=[vmem, vmem, pl.BlockSpec(memory_space=pltpu.SMEM)] + [hbm] * 5,
        out_specs=(vmem, vmem),
        scratch_shapes=[
            pltpu.VMEM((members, rows), bf16),
            pltpu.VMEM((width, rows), bf16),
            pltpu.VMEM((obs, BLK, BLK), bf16),
            pltpu.VMEM((obs, BLK), f32),
            pltpu.VMEM((obs, BLK), f32),
            pltpu.VMEM((width, members), bf16),
            pltpu.VMEM((slots, 8, BLK), jnp.int32),
            pltpu.VMEM((slots, obs, near), bf16),
            pltpu.VMEM((near, slots * obs), bf16),
            pltpu.VMEM((obs, slots * HB), bf16),
            pltpu.VMEM((slots * HB, obs), bf16),
            pltpu.VMEM((near, BLK), bf16),
            pltpu.VMEM((slots * HB, BLK), bf16),
            pltpu.VMEM((slots, obs, BLK), bf16),
            pltpu.VMEM((slots, obs, BLK), bf16),
            pltpu.VMEM((obs, BLK), bf16),
            pltpu.VMEM((slots * obs, BLK), bf16),
            pltpu.VMEM((slots * HB, BLK), bf16),
            pltpu.VMEM((slots, HB, BLK), bf16),
            pltpu.VMEM((HB, BLK), bf16),
            pltpu.VMEM((HB, BLK), bf16),
            pltpu.VMEM((blocks, BLK), f32),
            pltpu.VMEM((2, tiles // 2, 1, BLK), f32),
            pltpu.VMEM((tiles // 2, 1, BLK), f32),
            pltpu.VMEM((slots * tiles // 2, 1, BLK), f32),
            pltpu.SemaphoreType.DMA((11,)),
            sems(slots),
            sems(slots),
            sems(3),
            sems(slots),
            sems(slots),
            sems(slots),
            sems(slots * tiles // 2),
        ],
        compiler_params=pltpu.CompilerParams(
            collective_id=0, has_side_effects=True, vmem_limit_bytes=61 * 1024 * 1024
        ),
    )(
        control.reshape(-1, BLK),
        block_index,
        counts,
        anomalies[0],
        modes,
        interp[0],
        innovation[0],
        obs_weight[0],
    )
    gradient = grad[0, : control.shape[0] // tiles]
    return departure[None], gradient


def solution(mesh):
    in_specs = (
        P(),
        P("slot", None, "tile"),
        P(None, "tile"),
        P("slot", "tile", None, None),
        P("slot", "tile"),
        P("slot", "tile"),
        P("slot", "tile", None),
        P("slot", "tile", None),
    )
    out_specs = (P("slot", "tile", None), P("tile"))
    return jax.shard_map(
        functools.partial(on_device, mesh.shape["slot"], mesh.shape["tile"]),
        mesh=mesh,
        in_specs=in_specs,
        out_specs=out_specs,
        check_vma=False,
    )
```

```python
import functools

import jax
import jax.numpy as jnp
from jax import lax
from jax.experimental import pallas as pl
from jax.experimental.pallas import tpu as pltpu
from jax.sharding import PartitionSpec as P

BLK = 128
HB = 128
STEP = 16
MESH = pl.DeviceIdType.MESH
NT = (((1,), (1,)), ((), ()))


def kernel(
    slots,
    tiles,
    ctl_ref,
    idx_ref,
    cnt_ref,
    anom_hbm,
    modes_hbm,
    interp_hbm,
    innov_hbm,
    wt_hbm,
    dep_ref,
    grad_ref,
    anom,
    modes,
    interp,
    innov,
    wt,
    coarse,
    idxs,
    pick_hot,
    add_hot,
    edge_pick,
    edge_add,
    win,
    edges,
    picks,
    got,
    states,
    pulled,
    edge_out,
    edge_back,
    inner_out,
    inner_back,
    adj,
    gs,
    gp,
    gr,
    local_sem,
    idx_sem,
    edge_sem,
    core_sem,
    pick_sem,
    pull_sem,
    back_sem,
    g_sem,
):
    s = lax.axis_index("slot")
    t = lax.axis_index("tile")
    members, rows = anom.shape
    width = modes.shape[0]
    blocks = rows // BLK
    obs = interp.shape[0]
    reach = blocks + 2 * HB
    f32 = jnp.float32
    bf16 = jnp.bfloat16
    chips = tiles // 2
    z = t // 2
    core = lax.rem(t, 2)
    partner = (s, t + 1 - 2 * core)
    outer = lax.rem(t + tiles - 1 + 2 * core, tiles)
    halves = (core, 1 - core)

    def slot_plus(d, tile=None):
        return (lax.rem(s + d, slots), t if tile is None else tile)

    def slot_minus(d):
        return (lax.rem(s + slots - d, slots), t)

    def remote(src, dst, sems, i, target):
        return pltpu.make_async_remote_copy(
            src_ref=src,
            dst_ref=dst,
            send_sem=sems.at[0, i],
            recv_sem=sems.at[1, i],
            device_id=target,
            device_id_type=MESH,
        )

    barrier = pltpu.get_barrier_semaphore()
    pl.semaphore_signal(barrier, inc=1, device_id=partner, device_id_type=MESH)
    greeted = 1
    for d in range(slots):
        for e in range(chips):
            if d or e:
                to = (lax.rem(s + d, slots), lax.rem(z + e, chips) * 2 + core)
                pl.semaphore_signal(barrier, inc=1, device_id=to, device_id_type=MESH)
                greeted += 1
    for d in range(slots):
        pl.semaphore_signal(barrier, inc=1, device_id=slot_plus(d, outer), device_id_type=MESH)
        greeted += 1

    parts = 4
    part_rows = rows // parts
    starts = [
        pl.multiple_of(half * (rows // 2) + q * part_rows, part_rows)
        for half in halves
        for q in range(2)
    ]
    loads = []
    for c in range(parts):
        cols = pl.ds(starts[c], part_rows)
        pair = (
            pltpu.make_async_copy(modes_hbm.at[:, cols], modes.at[:, cols], local_sem.at[2 * c]),
            pltpu.make_async_copy(anom_hbm.at[:, cols], anom.at[:, cols], local_sem.at[2 * c + 1]),
        )
        for copy in pair:
            copy.start()
        loads.append(pair)
    base = 2 * parts
    load_interp = pltpu.make_async_copy(interp_hbm, interp, local_sem.at[base])
    load_innov = pltpu.make_async_copy(innov_hbm, innov, local_sem.at[base + 1])
    load_wt = pltpu.make_async_copy(wt_hbm, wt, local_sem.at[base + 2])
    load_interp.start()
    load_innov.start()
    load_wt.start()

    idxs[0] = jnp.broadcast_to(idx_ref[...], (8, BLK))

    per_row = BLK // width
    ctl = ctl_ref[...].astype(bf16)
    crows = ctl.shape[0]
    spread = (
        lax.broadcasted_iota(jnp.int32, (members, crows), 0) // per_row
        == lax.broadcasted_iota(jnp.int32, (members, crows), 1)
    )
    spread = jnp.where(spread, 1.0, 0.0).astype(bf16)
    wide = jnp.dot(spread, ctl, preferred_element_type=f32)
    lane = lax.broadcasted_iota(jnp.int32, (members, BLK), 1)
    member = lax.broadcasted_iota(jnp.int32, (members, BLK), 0)
    wide = jnp.where(lane // width == lax.rem(member, per_row), wide, 0.0).astype(bf16)
    fold = (
        lax.rem(lax.broadcasted_iota(jnp.int32, (width, BLK), 1), width)
        == lax.broadcasted_iota(jnp.int32, (width, BLK), 0)
    )
    fold = jnp.where(fold, 1.0, 0.0).astype(bf16)
    coarse[...] = lax.dot_general(fold, wide, NT, preferred_element_type=f32).astype(bf16)

    half_blocks = blocks // 2
    half_at = [pl.multiple_of(half * half_blocks, half_blocks) for half in halves]

    def increments(h, q):
        def body(i, carry):
            block = half_at[h] + q * (half_blocks // 2) + i * STEP
            block = pl.multiple_of(block, STEP)
            cols = pl.ds(pl.multiple_of(block * BLK, STEP * BLK), STEP * BLK)
            mixed = jnp.dot(coarse[...], anom[:, cols], preferred_element_type=f32)
            prod = mixed * modes[:, cols].astype(f32)
            sums = jnp.concatenate(
                [
                    jnp.sum(prod[:, j * BLK : (j + 1) * BLK], axis=0, keepdims=True)
                    for j in range(STEP)
                ],
                axis=0,
            )
            win[pl.ds(block, STEP), :] = sums.astype(bf16)
            return carry

        lax.fori_loop(0, half_blocks // 2 // STEP, body, 0, unroll=2)

    for q in range(2):
        for copy in loads[q]:
            copy.wait()
        increments(0, q)

    pl.semaphore_wait(barrier, greeted)

    idx_copies = []
    for d in range(1, slots):
        copy = remote(idxs.at[0], idxs.at[d], idx_sem, d, slot_plus(d))
        copy.start()
        idx_copies.append(copy)
    edge_copies = []
    for d in range(slots):
        copy = remote(
            win.at[pl.ds(half_at[0], HB)],
            edges.at[pl.ds(d * HB, HB)],
            edge_sem,
            d,
            slot_plus(d, outer),
        )
        copy.start()
        edge_copies.append(copy)

    for q in range(2):
        for copy in loads[2 + q]:
            copy.wait()
        increments(1, q)
    inner_copy = remote(
        win.at[pl.ds(half_at[1], HB)], win.at[pl.ds(blocks, HB)], core_sem, 0, partner
    )
    inner_copy.start()

    origin = s * reach
    outer_at = core * (HB + blocks)
    inner_at = HB + blocks - outer_at
    along = lax.broadcasted_iota(jnp.int32, (obs, BLK), 1)
    down = lax.broadcasted_iota(jnp.int32, (BLK, obs), 0)

    def hot(condition):
        return jnp.where(condition, 1.0, 0.0).astype(bf16)

    mine = jnp.broadcast_to(idxs[0, 0:1, :].astype(f32), (obs, BLK))
    mine_column = jnp.transpose(mine)
    for d in range(slots):
        at = lax.rem(s + slots - d, slots) * reach + outer_at
        edge_pick[:, d * HB : (d + 1) * HB] = hot(mine_column == (along + at).astype(f32))
        edge_add[d * HB : (d + 1) * HB, :] = hot(mine == (down + at).astype(f32))
    for d in range(slots):
        if d > 0:
            idx_copies[d - 1].wait_recv()
        listed = jnp.broadcast_to(idxs[d, 0:1, :].astype(f32), (obs, BLK))
        column = jnp.transpose(listed)
        for q in range(blocks // BLK + 1):
            at = origin + (HB + q * BLK if q < blocks // BLK else inner_at)
            pick_hot[d, :, q * BLK : (q + 1) * BLK] = hot(column == (along + at).astype(f32))
            add_hot[q * BLK : (q + 1) * BLK, d * obs : (d + 1) * obs] = hot(
                listed == (down + at).astype(f32)
            )

    inner_copy.wait_recv()
    pick_copies = []
    for d in range(1, slots):
        picks[d] = jnp.dot(pick_hot[d], win[...], preferred_element_type=f32).astype(bf16)
        copy = remote(picks.at[d], got.at[d], pick_sem, d, slot_minus(d))
        copy.start()
        pick_copies.append(copy)
    total = jnp.dot(pick_hot[0], win[...], preferred_element_type=f32)
    load_interp.wait()
    load_innov.wait()
    load_wt.wait()
    for copy in edge_copies:
        copy.wait_recv()
    total = total + jnp.dot(edge_pick[...], edges[...], preferred_element_type=f32)
    for d in range(1, slots):
        pick_copies[d - 1].wait_recv()
        total = total + got[d].astype(f32)
    states[...] = total.astype(bf16)

    live = cnt_ref[0, 0]
    sub = lax.broadcasted_iota(jnp.int32, (STEP, BLK), 0)

    def observe(g, carry):
        first = pl.multiple_of(g * STEP, STEP)
        mats = interp[pl.ds(first, STEP)].reshape(STEP * BLK, BLK)
        mapped_all = lax.dot_general(
            states[pl.ds(first, STEP), :], mats, NT, preferred_element_type=f32
        )
        mapped = mapped_all[:, 0:BLK]
        for r in range(1, STEP):
            mapped = jnp.where(sub == r, mapped_all[:, r * BLK : (r + 1) * BLK], mapped)
        misfit = jnp.where(
            sub + first < live, mapped - innov[pl.ds(first, STEP), :], jnp.zeros_like(mapped)
        )
        dep_ref[pl.ds(first, STEP), :] = misfit
        weighted = wt[pl.ds(first, STEP), :] * misfit
        spread_w = jnp.concatenate(
            [jnp.where(sub == r, weighted, 0.0).astype(bf16) for r in range(STEP)], axis=1
        )
        pulled[pl.ds(first, STEP), :] = jnp.dot(
            spread_w, mats, preferred_element_type=f32
        ).astype(bf16)
        return carry

    lax.fori_loop(0, obs // STEP, observe, 0, unroll=4)

    pull_copies = []
    for d in range(1, slots):
        copy = remote(
            pulled.at[pl.ds(0, obs)], pulled.at[pl.ds(d * obs, obs)], pull_sem, d, slot_plus(d)
        )
        copy.start()
        pull_copies.append(copy)
    edge_out[...] = jnp.dot(
        edge_add[...], pulled[0:obs, :], preferred_element_type=f32
    ).astype(bf16)
    back_copies = []
    for d in range(slots):
        copy = remote(
            edge_out.at[pl.ds(d * HB, HB)],
            edge_back.at[d],
            back_sem,
            d,
            (lax.rem(s + slots - d, slots), outer),
        )
        copy.start()
        back_copies.append(copy)
    for copy in pull_copies:
        copy.wait_recv()

    inner_out[...] = jnp.dot(
        add_hot[blocks : blocks + HB, :], pulled[...], preferred_element_type=f32
    ).astype(bf16)
    inner_send = remote(inner_out, inner_back, core_sem, 1, partner)
    inner_send.start()
    adj[...] = jnp.dot(add_hot[0:blocks, :], pulled[...], preferred_element_type=f32)
    def project(h):
        def body(i, acc):
            block = pl.multiple_of(half_at[h] + i * STEP, STEP)
            cols = pl.ds(pl.multiple_of(block * BLK, STEP * BLK), STEP * BLK)
            rows_adj = adj[pl.ds(block, STEP), :]
            part = modes[:, cols].astype(f32)
            scaled = jnp.concatenate(
                [
                    (part[:, j * BLK : (j + 1) * BLK] * rows_adj[j : j + 1, :]).astype(bf16)
                    for j in range(STEP)
                ],
                axis=1,
            )
            return acc + lax.dot_general(anom[:, cols], scaled, NT, preferred_element_type=f32)

        return body

    steps = half_blocks // STEP
    inner_send.wait_recv()
    inner_half = pl.ds(half_at[1], HB)
    adj[inner_half, :] = adj[inner_half, :] + inner_back[...].astype(f32)
    acc = lax.fori_loop(0, steps, project(1), jnp.zeros((members, width), f32), unroll=4)
    extra = None
    for d in range(slots):
        back_copies[d].wait_recv()
        got_edge = edge_back[d].astype(f32)
        extra = got_edge if extra is None else extra + got_edge
    outer_half = pl.ds(half_at[0], HB)
    adj[outer_half, :] = adj[outer_half, :] + extra
    acc = lax.fori_loop(0, steps, project(0), acc, unroll=4)

    share_rows = members // tiles
    wide = jnp.concatenate([acc] * per_row, axis=1)
    wide = jnp.where(lane // width == lax.rem(member, share_rows), wide, 0.0)
    for j in range(tiles):
        gs[j % 2, j // 2] = jnp.sum(
            wide[j * share_rows : (j + 1) * share_rows, :], axis=0, keepdims=True
        )

    core_send = remote(gs.at[1 - core], gp, core_sem, 2, partner)
    core_send.start()
    core_send.wait_recv()
    gs[core] = gs[core] + gp[...]
    g_copies = []
    for d in range(slots):
        for e in range(chips):
            if d or e:
                to = lax.rem(z + e, chips)
                i = d * chips + e
                copy = remote(
                    gs.at[core, to],
                    gr.at[i],
                    g_sem,
                    i,
                    (lax.rem(s + d, slots), to * 2 + core),
                )
                copy.start()
                g_copies.append(copy)

    share = members * width // tiles
    per_line = BLK // share
    line = ctl_ref[pl.ds(t // per_line, 1), :]
    own = line
    for q in range(1, per_line):
        moved = jnp.concatenate([line[:, q * share :], line[:, : q * share]], axis=1)
        own = jnp.where(lax.rem(t, per_line) == q, moved, own)

    result = gs[core, z]
    for copy in g_copies:
        copy.wait_recv()
    for i in range(1, slots * chips):
        result = result + gr[i]
    grad_ref[...] = own + result

    for copy in (
        idx_copies
        + edge_copies
        + [inner_copy]
        + pick_copies
        + pull_copies
        + back_copies
        + [inner_send, core_send]
        + g_copies
    ):
        copy.wait_send()


def on_device(
    slots, tiles, control, anomalies, modes, interp, block_index, counts, innovation, obs_weight
):
    members, rows = anomalies.shape[1:]
    width = modes.shape[0]
    obs = interp.shape[1]
    blocks = rows // BLK
    near = blocks + HB
    f32 = jnp.float32
    bf16 = jnp.bfloat16
    vmem = pl.BlockSpec(memory_space=pltpu.VMEM)
    hbm = pl.BlockSpec(memory_space=pl.ANY)

    def sems(n):
        return pltpu.SemaphoreType.DMA((2, n))

    departure, grad = pl.pallas_call(
        functools.partial(kernel, slots, tiles),
        out_shape=(
            pltpu.VMEM((obs, BLK), f32),
            pltpu.VMEM((1, BLK), f32),
        ),
        in_specs=[vmem, vmem, pl.BlockSpec(memory_space=pltpu.SMEM)] + [hbm] * 5,
        out_specs=(vmem, vmem),
        scratch_shapes=[
            pltpu.VMEM((members, rows), bf16),
            pltpu.VMEM((width, rows), bf16),
            pltpu.VMEM((obs, BLK, BLK), bf16),
            pltpu.VMEM((obs, BLK), f32),
            pltpu.VMEM((obs, BLK), f32),
            pltpu.VMEM((width, members), bf16),
            pltpu.VMEM((slots, 8, BLK), jnp.int32),
            pltpu.VMEM((slots, obs, near), bf16),
            pltpu.VMEM((near, slots * obs), bf16),
            pltpu.VMEM((obs, slots * HB), bf16),
            pltpu.VMEM((slots * HB, obs), bf16),
            pltpu.VMEM((near, BLK), bf16),
            pltpu.VMEM((slots * HB, BLK), bf16),
            pltpu.VMEM((slots, obs, BLK), bf16),
            pltpu.VMEM((slots, obs, BLK), bf16),
            pltpu.VMEM((obs, BLK), bf16),
            pltpu.VMEM((slots * obs, BLK), bf16),
            pltpu.VMEM((slots * HB, BLK), bf16),
            pltpu.VMEM((slots, HB, BLK), bf16),
            pltpu.VMEM((HB, BLK), bf16),
            pltpu.VMEM((HB, BLK), bf16),
            pltpu.VMEM((blocks, BLK), f32),
            pltpu.VMEM((2, tiles // 2, 1, BLK), f32),
            pltpu.VMEM((tiles // 2, 1, BLK), f32),
            pltpu.VMEM((slots * tiles // 2, 1, BLK), f32),
            pltpu.SemaphoreType.DMA((11,)),
            sems(slots),
            sems(slots),
            sems(3),
            sems(slots),
            sems(slots),
            sems(slots),
            sems(slots * tiles // 2),
        ],
        compiler_params=pltpu.CompilerParams(
            collective_id=0, has_side_effects=True, vmem_limit_bytes=61 * 1024 * 1024
        ),
    )(
        control.reshape(-1, BLK),
        block_index,
        counts,
        anomalies[0],
        modes,
        interp[0],
        innovation[0],
        obs_weight[0],
    )
    gradient = grad[0, : control.shape[0] // tiles]
    return departure[None], gradient


def solution(mesh):
    in_specs = (
        P(),
        P("slot", None, "tile"),
        P(None, "tile"),
        P("slot", "tile", None, None),
        P("slot", "tile"),
        P("slot", "tile"),
        P("slot", "tile", None),
        P("slot", "tile", None),
    )
    out_specs = (P("slot", "tile", None), P("tile"))
    return jax.shard_map(
        functools.partial(on_device, mesh.shape["slot"], mesh.shape["tile"]),
        mesh=mesh,
        in_specs=in_specs,
        out_specs=out_specs,
        check_vma=False,
    )
```
